128 devices in a mesh: grp: 8 (over y, core), sp: 16 (over x, z).
Axes of the slice: x: 4, y: 4, z: 4, core: 2. Of those that a mesh axis runs over, the one named last changes fastest.
Arguments:
- frames: bfloat16 [16, 4, 32, 240, 384], P('grp', None, 'sp'), may hold values from -6 to 6
- conv_weight: bfloat16 [3, 3, 3, 384, 384], replicated, may hold values from -0.0625 to 0.0625
- conv_bias: float32 [384], replicated, may hold values from -4 to 4
- projection: bfloat16 [384, 16], replicated, may hold values from -0.3125 to 0.3125
Outputs:
- coded: bfloat16 [16, 16, 2, 240, 32], P('grp', None, None, 'sp')
The draws below stay inside these ranges and needn't reach their ends.
All inputs are finite; a program needn't handle non-finite values.
Results may differ from the reference program's by a relative error of at most 0.0065.
Values may be sent and summed in bfloat16 or wider, within the bound.
No kernel may reach another device: no remote copies, remote signals or barrier semaphores. Data moves between devices by JAX's collectives and lax.ppermute only.
A program may use at most 192 MiB of HBM per device.

```python
import jax
import jax.numpy as jnp
from jax import lax

CH = 384
LAT = 16
FR = 2
COLS = 240
CLIPS = 16
NH = 32


def steps_of(key, extent, shards, low, top_value):
    def one(axis_at, blocks):
        heights = jax.random.uniform(jax.random.fold_in(jax.random.fold_in(key, 6), axis_at), (blocks,), jnp.float32, low / len(shards), top_value / len(shards))
        return jnp.repeat(jnp.exp(heights), extent[axis_at] // blocks).reshape((-1,) + (1,) * (len(extent) - axis_at - 1))

    gain = one(*shards[0])
    for cut in shards[1:]:
        gain = gain * one(*cut)
    return gain


def normal_values(own_key, shape, deviation, limit, shards=(), kind=jnp.bfloat16):
    loudness = steps_of(own_key, shape, shards, -0.22, 0.18) if shards else 1.0
    result = jax.random.normal(own_key, shape, jnp.float32) * deviation * loudness
    return jnp.minimum(jnp.maximum(result, -limit), limit).astype(kind)


def setup_inputs(seed: int = 0) -> dict:
    splits = jax.random.split(jax.random.key(seed), 5)
    frames = normal_values(splits[0], (CLIPS, FR + 2, NH, COLS, CH), 1.0, 6.0, ((0, 8), (2, 16)))
    conv_weight = normal_values(splits[1], (3, 3, 3, CH, CH), (27 * CH) ** -0.5, 0.0625)
    conv_bias = normal_values(splits[2], (CH,), 1.0, 4.0, (), jnp.float32)
    projection = normal_values(splits[3], (CH, LAT), CH ** -0.5, 0.3125)
    return dict(frames=frames, conv_weight=conv_weight, conv_bias=conv_bias, projection=projection)


def encode_clip(clip, conv_weight, conv_bias, projection):
    padded = jnp.pad(clip, ((0, 0), (1, 1), (1, 1), (0, 0)))
    total = jnp.zeros((FR * NH * COLS, CH), jnp.float32)
    for time_tap in range(3):
        for row_tap in range(3):
            for col_tap in range(3):
                piece = padded[time_tap:time_tap + FR, row_tap:row_tap + NH, col_tap:col_tap + COLS].reshape(-1, CH)
                total = total + jnp.dot(piece, conv_weight[time_tap, row_tap, col_tap], preferred_element_type=jnp.float32)
    hidden = jax.nn.silu(total + conv_bias).astype(jnp.bfloat16)
    latent = jnp.dot(hidden, projection, preferred_element_type=jnp.float32)
    return latent.reshape(FR, NH, COLS, LAT)


def reference(frames, conv_weight, conv_bias, projection):
    latent = lax.map(lambda clip: encode_clip(clip, conv_weight, conv_bias, projection), frames)
    lowest = jnp.min(latent, axis=(0, 1, 2, 3))
    highest = jnp.max(latent, axis=(0, 1, 2, 3))
    coded = ((latent - lowest) / (highest - lowest) * 2.0 - 1.0).astype(jnp.bfloat16)
    return jnp.transpose(coded, (0, 4, 1, 3, 2))
```

```python
import jax
import jax.numpy as jnp
from jax import lax
from jax.experimental import pallas as pl
from jax.experimental.pallas import tpu as pltpu
from jax.sharding import PartitionSpec as P

F32, BF16 = jnp.float32, jnp.bfloat16
HBM, VMEM = pltpu.MemorySpace.HBM, pltpu.MemorySpace.VMEM


def dot(a, b):
    return jnp.dot(a, b, preferred_element_type=F32)


def cost(macs, nbytes):
    return pl.CostEstimate(flops=2 * macs, bytes_accessed=nbytes, transcendentals=0)


def params(mib):
    return pltpu.CompilerParams(vmem_limit_bytes=mib * 2**20)


def spread_taps(x, taps, at):
    cols, chans = x.shape
    wide = x.astype(F32)
    col = lax.broadcasted_iota(jnp.int32, wide.shape, 0)
    before = jnp.where(col == 0, 0.0, pltpu.roll(wide, 1, 0)).astype(BF16)
    after = jnp.where(col == cols - 1, 0.0, pltpu.roll(wide, cols - 1, 0)).astype(BF16)
    base = at * 3 * chans
    taps[:, base : base + chans] = before
    taps[:, base + chans : base + 2 * chans] = x
    taps[:, base + 2 * chans : base + 3 * chans] = after


def edge_sums(frames, weight, row, row_tap):
    clips, depth, _, cols, ch = frames.shape

    def kernel(x_hbm, w_hbm, o_ref, x, w, taps, x_sem, w_sem):
        in_x = [pltpu.make_async_copy(x_hbm.at[c, :, row], x.at[c], x_sem.at[c]) for c in range(clips)]
        in_w = [
            pltpu.make_async_copy(w_hbm.at[a, row_tap], w.at[:, :, pl.ds((2 - a) * ch, ch)], w_sem.at[a])
            for a in range(3)
        ]
        in_x[0].start()
        for a in range(3):
            in_w[a].start()
        for c in range(1, clips):
            in_x[c].start()
        for c in range(clips):
            in_x[c].wait()
            for f in range(depth):
                spread_taps(x[c, f], taps.at[c], f)
            if c == 0:
                for a in range(3):
                    in_w[a].wait()

            def term(f, low, high):
                return dot(
                    taps[c, :, f * 3 * ch : (f + 1) * 3 * ch],
                    w[:, :, low * ch : high * ch].reshape(3 * ch, (high - low) * ch),
                )

            both = term(1, 1, 3) + term(2, 0, 2)
            o_ref[c, 0] = (both[:, :ch] + term(0, 2, 3)).astype(BF16)
            o_ref[c, 1] = (both[:, ch:] + term(3, 0, 1)).astype(BF16)

    return pl.pallas_call(
        kernel,
        in_specs=[pl.BlockSpec(memory_space=HBM)] * 2,
        out_specs=pl.BlockSpec(memory_space=VMEM),
        out_shape=jax.ShapeDtypeStruct((clips, 2, cols, ch), BF16),
        scratch_shapes=[
            pltpu.VMEM((clips, depth, cols, ch), BF16),
            pltpu.VMEM((3, ch, 3 * ch), BF16),
            pltpu.VMEM((clips, cols, depth * 3 * ch), BF16),
            pltpu.SemaphoreType.DMA((clips,)),
            pltpu.SemaphoreType.DMA((3,)),
        ],
        compiler_params=params(60),
        cost_estimate=cost(clips * 2 * cols * 9 * ch * ch, 5 * 10**6),
    )(frames, weight)


def inner_sums(frames, weight):
    clips, depth, rows, cols, ch = frames.shape

    def kernel(x_hbm, w_hbm, o_hbm, x, w, taps, out, x_sem, w_sem, o_sem):
        in_x = [pltpu.make_async_copy(x_hbm.at[c], x.at[c], x_sem.at[c]) for c in range(clips)]
        in_w = [
            pltpu.make_async_copy(w_hbm.at[a, b], w.at[a, :, :, pl.ds((2 - b) * ch, ch)], w_sem.at[a, b])
            for a in range(3)
            for b in (1, 0, 2)
        ]
        in_x[0].start()
        for copy in in_w:
            copy.start()
        for c in range(1, clips):
            in_x[c].start()
        outs = []
        for c in range(clips):
            in_x[c].wait()
            for r in range(rows):
                for f in range(depth):
                    spread_taps(x[c, f, r], taps.at[c, r], f)
            if c == 0:
                for copy in in_w:
                    copy.wait()
            for t in range(2):
                window = slice(t * 3 * ch, (t + 3) * 3 * ch)
                out[c, t] = dot(taps[c, 0, :, window], w[:, :, :, ch:].reshape(9 * ch, 2 * ch)) + dot(
                    taps[c, 1, :, window], w[:, :, :, : 2 * ch].reshape(9 * ch, 2 * ch)
                )
                copy = pltpu.make_async_copy(out.at[c, t], o_hbm.at[c, t], o_sem.at[c, t])
                copy.start()
                outs.append(copy)
        for copy in outs:
            copy.wait()

    return pl.pallas_call(
        kernel,
        in_specs=[pl.BlockSpec(memory_space=HBM)] * 2,
        out_specs=pl.BlockSpec(memory_space=HBM),
        out_shape=jax.ShapeDtypeStruct((clips, 2, cols, rows * ch), F32),
        scratch_shapes=[
            pltpu.VMEM((clips, depth, rows, cols, ch), BF16),
            pltpu.VMEM((3, 3, ch, 3 * ch), BF16),
            pltpu.VMEM((clips, rows, cols, depth * 3 * ch), BF16),
            pltpu.VMEM((clips, 2, cols, rows * ch), F32),
            pltpu.SemaphoreType.DMA((clips,)),
            pltpu.SemaphoreType.DMA((3, 3)),
            pltpu.SemaphoreType.DMA((clips, 2)),
        ],
        compiler_params=params(60),
        cost_estimate=cost(clips * 2 * cols * 36 * ch * ch, 14 * 10**6),
    )(frames, weight)


def latent_messages(sums, from_above, from_below, bias, placed, shards):
    clips, outs, cols, wide = sums.shape
    ch = wide // 2
    lanes = placed.shape[1]
    half = lanes // 2
    share = cols // shards

    def over_channels(x, pick):
        x = pick(x, pltpu.roll(x, half // 2, 1))
        lane = lax.broadcasted_iota(jnp.int32, x.shape, 1)
        return pick(x, jnp.where(lane % 2 == 0, pltpu.roll(x, lanes - 1, 1), pltpu.roll(x, 1, 1)))

    def kernel(s_ref, above_ref, below_ref, b_ref, p_ref, o_ref, hidden, latent):
        bias_row = b_ref[...]
        lowest = highest = None
        for r, halo in ((1, below_ref), (0, above_ref)):
            for c in range(clips):
                for t in range(outs):
                    v = s_ref[c, t, :, r * ch : (r + 1) * ch] + halo[c, t].astype(F32) + bias_row
                    v = v * 0.5
                    at = (c * outs + t) * ch
                    hidden[:, at : at + ch] = (v + v * jnp.tanh(v)).astype(BF16)
            found = dot(hidden[...], p_ref[...])
            latent[r, :cols] = found
            latent[r, cols:] = jnp.zeros_like(latent[r, cols:])
            low = jnp.min(found, axis=0, keepdims=True)
            high = jnp.max(found, axis=0, keepdims=True)
            lowest = low if lowest is None else jnp.minimum(lowest, low)
            highest = high if highest is None else jnp.maximum(highest, high)
        lowest = over_channels(lowest, jnp.minimum)
        highest = over_channels(highest, jnp.maximum)
        at_end = (lax.broadcasted_iota(jnp.int32, (8, lanes), 0) == 7) & (
            lax.broadcasted_iota(jnp.int32, (8, lanes), 1) >= half
        )
        in_front = lax.broadcasted_iota(jnp.int32, (8, lanes), 1) < half
        for s in range(shards):
            for r, extreme in ((0, lowest), (1, highest)):
                first = latent[r, pl.ds(share * s, 8)]
                second = latent[r, pl.ds(share * s + 8, 8)]
                o_ref[s, r * 8 : (r + 1) * 8] = jnp.where(at_end, extreme, jnp.where(in_front, first, second))

    return pl.pallas_call(
        kernel,
        in_specs=[pl.BlockSpec(memory_space=VMEM)] * 5,
        out_specs=pl.BlockSpec(memory_space=VMEM),
        out_shape=jax.ShapeDtypeStruct((shards, 16, lanes), F32),
        scratch_shapes=[pltpu.VMEM((cols, clips * outs * ch), BF16), pltpu.VMEM((2, cols + 8, lanes), F32)],
        compiler_params=params(50),
        cost_estimate=cost(2 * cols * clips * outs * ch * lanes, 4 * 10**6),
    )(sums, from_above, from_below, bias, placed)


def extremes(received, groups):
    lanes = received.shape[-1]

    def kernel(x_ref, o_ref):
        lane = lax.broadcasted_iota(jnp.int32, (1, lanes), 1)
        low = jnp.min(x_ref[:, 7, :], axis=0, keepdims=True)
        high = jnp.max(x_ref[:, 15, :], axis=0, keepdims=True)
        low = jnp.where(lane < lanes // 2, pltpu.roll(low, lanes // 2, 1), low)
        high = jnp.where(lane < lanes // 2, pltpu.roll(high, lanes // 2, 1), high)
        row = lax.broadcasted_iota(jnp.int32, (8, lanes), 0)
        both = jnp.where(row == 0, low, high)
        for g in range(groups):
            o_ref[g] = both

    return pl.pallas_call(
        kernel,
        in_specs=[pl.BlockSpec(memory_space=VMEM)],
        out_specs=pl.BlockSpec(memory_space=VMEM),
        out_shape=jax.ShapeDtypeStruct((groups, 8, lanes), F32),
    )(received)


def coded_columns(received, ranges, share):
    shards, _, lanes = received.shape
    half = lanes // 2

    def kernel(x_ref, g_ref, o_ref, coded, turned):
        low = jnp.min(g_ref[:, 0, :], axis=0, keepdims=True)
        high = jnp.max(g_ref[:, 1, :], axis=0, keepdims=True)
        x = x_ref[...].reshape(shards * 16, lanes)
        coded[...] = (x - low) / (high - low) * 2.0 - 1.0
        for w in range(8):
            block = coded[pl.ds(w, 2 * shards, stride=8), :].T
            turned[pl.ds(w, half, stride=16), :] = block[:half]
            turned[pl.ds(w + 8, half, stride=16), :] = block[half:]
        o_ref[...] = turned[...].reshape(half, 16, 2 * shards)[:, :share].astype(BF16)

    return pl.pallas_call(
        kernel,
        in_specs=[pl.BlockSpec(memory_space=VMEM)] * 2,
        out_specs=pl.BlockSpec(memory_space=VMEM),
        out_shape=jax.ShapeDtypeStruct((half, share, 2 * shards), BF16),
        scratch_shapes=[pltpu.VMEM((shards * 16, lanes), F32), pltpu.VMEM((half * 16, 2 * shards), F32)],
    )(received, ranges)


def on_device(frames, conv_weight, conv_bias, projection):
    clips, depth, rows, cols, ch = frames.shape
    latents = projection.shape[1]
    outs = depth - 2
    shards, groups = lax.axis_size("sp"), lax.axis_size("grp")
    forward = [(i, i + 1) for i in range(shards - 1)]
    backward = [(i + 1, i) for i in range(shards - 1)]

    from_below = lax.ppermute(edge_sums(frames, conv_weight, 0, 2), "sp", backward)
    from_above = lax.ppermute(edge_sums(frames, conv_weight, rows - 1, 0), "sp", forward)
    sums = inner_sums(frames, conv_weight)

    eye_c, eye_t = jnp.eye(clips, dtype=BF16), jnp.eye(outs, dtype=BF16)
    placed = jnp.einsum("ik,cd,tu->ctidku", projection, eye_c, eye_t)
    placed = placed.reshape(clips * outs * ch, clips * latents * outs)
    placed = jnp.concatenate([placed, placed], axis=1)

    messages = latent_messages(sums, from_above, from_below, conv_bias.reshape(1, ch), placed, shards)
    received = lax.all_to_all(messages, "sp", 0, 0)
    ranges = lax.all_to_all(extremes(received, groups), "grp", 0, 0)
    coded = coded_columns(received, ranges, cols // shards)
    return coded.reshape(clips, latents, outs, cols // shards, rows * shards)


def solution(mesh):
    placed = (P("grp", None, "sp", None, None), P(), P(), P())
    return jax.shard_map(
        on_device,
        mesh=mesh,
        in_specs=placed,
        out_specs=P("grp", None, None, "sp", None),
        check_vma=False,
    )
```

```python
import functools

import jax
import jax.numpy as jnp
from jax import lax
from jax.experimental import pallas as pl
from jax.experimental.pallas import tpu as pltpu
from jax.sharding import PartitionSpec as P

F32, BF16 = jnp.float32, jnp.bfloat16
HBM, VMEM = pltpu.MemorySpace.HBM, pltpu.MemorySpace.VMEM
IN_HBM, IN_VMEM = pl.BlockSpec(memory_space=HBM), pl.BlockSpec(memory_space=VMEM)
DMA = pltpu.SemaphoreType.DMA


def dot(a, b):
    return jnp.dot(a, b, preferred_element_type=F32)


def cost(macs, nbytes):
    return pl.CostEstimate(flops=2 * macs, bytes_accessed=nbytes, transcendentals=0)


def params(mib):
    return pltpu.CompilerParams(vmem_limit_bytes=mib * 2**20)


def spread_taps(x, taps, at):
    cols, chans = x.shape
    wide = x.astype(F32)
    col = lax.broadcasted_iota(jnp.int32, wide.shape, 0)
    before = jnp.where(col == 0, 0.0, pltpu.roll(wide, 1, 0)).astype(BF16)
    after = jnp.where(col == cols - 1, 0.0, pltpu.roll(wide, cols - 1, 0)).astype(BF16)
    base = at * 3 * chans
    taps[:, base : base + chans] = before
    taps[:, base + chans : base + 2 * chans] = x
    taps[:, base + 2 * chans : base + 3 * chans] = after


def in_hbm(*arrays):
    return [pltpu.with_memory_space_constraint(x, HBM) for x in arrays]


def in_vmem(x):
    return pltpu.with_memory_space_constraint(x, VMEM)


def odd_device():
    return lax.rem(lax.axis_index("sp"), 2)


def edge_terms(taps, w, o_ref):
    ch = w.shape[1]

    def term(f, low, high):
        return dot(
            taps[:, f * 3 * ch : (f + 1) * 3 * ch],
            w[:, :, low * ch : high * ch].reshape(3 * ch, (high - low) * ch),
        )

    both = term(1, 1, 3) + term(2, 0, 2)
    o_ref[0] = (both[:, :ch] + term(0, 2, 3)).astype(BF16)
    o_ref[1] = (both[:, ch:] + term(3, 0, 1)).astype(BF16)


def edge_sums(frames, weight, projection):
    clips, depth, rows, cols, ch = frames.shape
    latents = projection.shape[0]

    def kernel(
        x_hbm, w_hbm, p_hbm, near_ref, far_ref, near_taps, far_taps, inner, placed, x, w, p, x_sem, w_sem, i_sem, p_sem
    ):
        odd = odd_device()
        in_p = pltpu.make_async_copy(p_hbm, p, p_sem)
        in_x, in_w = [], []
        for e, (row, tap) in enumerate(((1 - odd, 2 * odd), (odd, 2 - 2 * odd))):
            in_x.append(
                [pltpu.make_async_copy(x_hbm.at[c, :, row], x.at[e, c], x_sem.at[e, c]) for c in range(clips)]
            )
            in_w.append(
                [
                    pltpu.make_async_copy(w_hbm.at[a, tap], w.at[e, :, :, pl.ds((2 - a) * ch, ch)], w_sem.at[e, a])
                    for a in range(3)
                ]
            )
        in_inner = [
            pltpu.make_async_copy(w_hbm.at[a, b], inner.at[a, :, :, pl.ds(place * ch, ch)], i_sem.at[a, place])
            for a in range(3)
            for place, b in enumerate((2 * odd, 1, 2 - 2 * odd))
        ]
        in_x[0][0].start()
        for copy in in_w[0]:
            copy.start()
        in_x[0][1].start()
        in_p.start()
        in_x[0][0].wait()
        for f in range(depth):
            spread_taps(x[0, 0, f], near_taps.at[0], f)
        in_p.wait()
        k = lax.broadcasted_iota(jnp.int32, (latents, 128), 0)
        lane = lax.broadcasted_iota(jnp.int32, (latents, 128), 1)
        for c in range(clips):
            for t in range(2):
                pick = (lane % 64 == t * 32 + c * latents + k).astype(F32).astype(BF16)
                turned = lax.dot_general(p[...], pick, (((0,), (0,)), ((), ())), preferred_element_type=F32)
                at = (c * 2 + t) * ch
                placed[at : at + ch] = turned.astype(BF16)
        for copy in in_w[0]:
            copy.wait()
        for copy in in_x[1] + in_w[1] + in_inner:
            copy.start()
        for e, (taps, o_ref) in enumerate(((near_taps, near_ref), (far_taps, far_ref))):
            for c in range(clips):
                if e + c > 0:
                    in_x[e][c].wait()
                    for f in range(depth):
                        spread_taps(x[e, c, f], taps.at[c], f)
                if e == 1 and c == 0:
                    for copy in in_w[e]:
                        copy.wait()
                edge_terms(taps.at[c], w.at[e], o_ref.at[c])
        for copy in in_inner:
            copy.wait()

    edge = jax.ShapeDtypeStruct((clips, 2, cols, ch), BF16)
    taps = pltpu.VMEM((clips, cols, depth * 3 * ch), BF16)
    return pl.pallas_call(
        kernel,
        in_specs=[IN_HBM] * 3,
        out_specs=[IN_VMEM] * 6,
        out_shape=[edge, edge, taps, taps, pltpu.VMEM((3, 3, ch, 3 * ch), BF16), pltpu.VMEM((4 * ch, 128), BF16)],
        scratch_shapes=[
            pltpu.VMEM((rows, clips, depth, cols, ch), BF16),
            pltpu.VMEM((rows, 3, ch, 3 * ch), BF16),
            pltpu.VMEM((latents, ch), BF16),
            DMA((rows, clips)),
            DMA((rows, 3)),
            DMA((3, 3)),
            DMA,
        ],
        compiler_params=params(20),
        cost_estimate=cost(clips * 4 * cols * 9 * ch * ch, 16 * 10**6),
    )(*in_hbm(frames, weight, projection))


def inner_sums(near, far, weight):
    clips, cols, _ = near.shape
    ch = weight.shape[2]

    def kernel(near, far, w, out):
        for c in range(clips):
            for t in range(2):
                window = slice(t * 3 * ch, (t + 3) * 3 * ch)
                out[c, t] = dot(near[c, :, window], w[:, :, :, ch:].reshape(9 * ch, 2 * ch)) + dot(
                    far[c, :, window], w[:, :, :, : 2 * ch].reshape(9 * ch, 2 * ch)
                )

    return pl.pallas_call(
        kernel,
        in_specs=[IN_VMEM] * 3,
        out_specs=IN_VMEM,
        out_shape=pltpu.VMEM((clips, 2, cols, 2 * ch), F32),
        compiler_params=params(16),
        cost_estimate=cost(clips * 8 * cols * 9 * ch * ch, 14 * 10**6),
    )(near, far, weight)


def latent_messages(sums, near, far, bias, placed, shards, groups):
    clips, outs, cols, wide = sums.shape
    ch = wide // 2
    lanes = placed.shape[1]
    half = lanes // 2
    share = cols // shards

    def over_channels(x, pick):
        x = pick(x, pltpu.roll(x, half // 4, 1))
        return pick(x, pltpu.roll(x, half // 2, 1))

    def in_terms(x):
        first = x.astype(BF16).astype(F32)
        second = (x - first).astype(BF16).astype(F32)
        third = x - first - second
        block = lax.broadcasted_iota(jnp.int32, x.shape, 1) // (half // 4)
        return jnp.where(block == 4, first, jnp.where(block == 5, second, jnp.where(block == 6, third, 0.0)))

    def kernel(s_ref, near_ref, far_ref, b_ref, p_ref, o_ref, hidden, latent):
        odd = odd_device()
        bias_row = b_ref[...]
        lowest = highest = None
        for part, (halo, row) in enumerate(((near_ref, 1 - odd), (far_ref, odd))):
            for c in range(clips):
                for t in range(outs):
                    v = s_ref[c, t, :, part * ch : (part + 1) * ch] + halo[c, t].astype(F32) + bias_row
                    v = v * 0.5
                    at = (c * outs + t) * ch
                    hidden[:, at : at + ch] = (v + v * jnp.tanh(v)).astype(BF16)
            found = dot(hidden[...], p_ref[...])
            latent[row, :cols] = found
            low = jnp.min(found, axis=0, keepdims=True)
            high = jnp.max(found, axis=0, keepdims=True)
            lowest = low if lowest is None else jnp.minimum(lowest, low)
            highest = high if highest is None else jnp.maximum(highest, high)
        latent[:, cols:] = jnp.zeros_like(latent[:, cols:])
        lowest = over_channels(lowest, jnp.minimum)
        highest = over_channels(highest, jnp.maximum)
        middle = (lowest + highest) * 0.5
        at_end = (lax.broadcasted_iota(jnp.int32, (8, lanes), 0) == 7) & (
            lax.broadcasted_iota(jnp.int32, (8, lanes), 1) >= half
        )
        in_front = lax.broadcasted_iota(jnp.int32, (8, lanes), 1) < half
        ends = (in_terms(lowest), in_terms(highest))
        for s in range(shards):
            rows = []
            for r in range(2):
                first = latent[r, pl.ds(share * s, 8)]
                second = latent[r, pl.ds(share * s + 8, 8)]
                rows.append(jnp.where(at_end, ends[r], jnp.where(in_front, first, second) - middle))
            message = jnp.concatenate(rows, axis=0).astype(BF16)
            for g in range(groups):
                o_ref[g, s] = message

    return pl.pallas_call(
        kernel,
        in_specs=[IN_VMEM] * 5,
        out_specs=IN_VMEM,
        out_shape=pltpu.VMEM((groups, shards, 16, lanes), BF16),
        scratch_shapes=[pltpu.VMEM((cols, clips * outs * ch), BF16), pltpu.VMEM((2, cols + 8, lanes), F32)],
        compiler_params=params(16),
        cost_estimate=cost(2 * cols * clips * outs * ch * lanes, 4 * 10**6),
    )(sums, near, far, bias, placed)


def coded_columns(received, share):
    groups, shards, _, lanes = received.shape
    latents = lanes // 8
    channels = lanes // 4

    def kernel(x_ref, o_ref, coded, turned):
        block = lax.broadcasted_iota(jnp.int32, (1, lanes), 1) // latents

        def end(g, row):
            terms = x_ref[g].astype(F32)[:, row, :]
            return terms + pltpu.roll(terms, lanes - latents, 1) + pltpu.roll(terms, lanes - 2 * latents, 1)

        def to_all(x):
            x = jnp.where(block == 4, x, 0.0)
            for step in (1, 2, 4):
                x = x + pltpu.roll(x, step * latents, 1)
            return x

        lows = [end(g, 7) for g in range(groups)]
        highs = [end(g, 15) for g in range(groups)]
        low = jnp.min(functools.reduce(jnp.minimum, lows), axis=0, keepdims=True)
        high = jnp.max(functools.reduce(jnp.maximum, highs), axis=0, keepdims=True)
        low, high = to_all(low), to_all(high)
        mine = lax.axis_index("grp")
        middle = to_all((end(mine, 7) + end(mine, 15)) * 0.5)
        x = x_ref[mine].astype(F32) + middle[:, None, :]
        coded[...] = ((x - low) / (high - low) * 2.0 - 1.0).reshape(shards * 16, lanes)
        for first in range(8):
            piece_of = coded[pl.ds(first, 2 * shards, stride=8), :].T
            for piece in range(4):
                w, t = first + 8 * (piece // 2), piece % 2
                if w < share:
                    rows = piece_of[piece * channels : (piece + 1) * channels]
                    turned[pl.ds(2 * w + t, channels, stride=2 * share), :] = rows
        o_ref[...] = turned[...].astype(BF16)

    return pl.pallas_call(
        kernel,
        in_specs=[IN_VMEM],
        out_specs=IN_VMEM,
        out_shape=jax.ShapeDtypeStruct((channels * share * 2, 2 * shards), BF16),
        scratch_shapes=[pltpu.VMEM((shards * 16, lanes), F32), pltpu.VMEM((channels * share * 2, 2 * shards), F32)],
        compiler_params=params(16),
    )(in_vmem(received))


def on_device(frames, conv_weight, conv_bias, projection):
    clips, depth, rows, cols, ch = frames.shape
    latents = projection.shape[1]
    outs = depth - 2
    shards, groups = lax.axis_size("sp"), lax.axis_size("grp")
    share = cols // shards

    def swap(x, first):
        pairs = [(i, i + 1) for i in range(first, shards - 1, 2)]
        return lax.ppermute(x, "sp", pairs + [(b, a) for a, b in pairs])

    near_sums, far_sums, near_taps, far_taps, inner_w, placed = edge_sums(frames, conv_weight, projection.T)
    near, far = swap(near_sums, 0), swap(far_sums, 1)
    sums = inner_sums(near_taps, far_taps, inner_w)

    messages = latent_messages(sums, near, far, conv_bias.reshape(1, ch), placed, shards, groups)
    messages = messages.reshape(groups * shards, 16, messages.shape[-1])
    received = lax.all_to_all(messages, ("grp", "sp"), 0, 0).reshape(groups, shards, 16, -1)
    coded = coded_columns(received, share)
    return coded.reshape(clips, latents, share, outs, rows * shards).transpose(0, 1, 3, 2, 4)


def solution(mesh):
    placed = (P("grp", None, "sp", None, None), P(), P(), P())
    return jax.shard_map(
        on_device,
        mesh=mesh,
        in_specs=placed,
        out_specs=P("grp", None, None, "sp", None),
        check_vma=False,
    )
```

```python
import functools

import jax
import jax.numpy as jnp
from jax import lax
from jax.experimental import pallas as pl
from jax.experimental.pallas import tpu as pltpu
from jax.sharding import PartitionSpec as P

F32, BF16 = jnp.float32, jnp.bfloat16
HBM, VMEM = pltpu.MemorySpace.HBM, pltpu.MemorySpace.VMEM
IN_HBM, IN_VMEM = pl.BlockSpec(memory_space=HBM), pl.BlockSpec(memory_space=VMEM)
DMA = pltpu.SemaphoreType.DMA


def dot(a, b):
    return jnp.dot(a, b, preferred_element_type=F32)


def cost(macs, nbytes):
    return pl.CostEstimate(flops=2 * macs, bytes_accessed=nbytes, transcendentals=0)


def params(mib):
    return pltpu.CompilerParams(vmem_limit_bytes=mib * 2**20)


def spread_taps(x, taps, at):
    cols, chans = x.shape
    wide = x.astype(F32)
    col = lax.broadcasted_iota(jnp.int32, wide.shape, 0)
    before = jnp.where(col == 0, 0.0, pltpu.roll(wide, 1, 0)).astype(BF16)
    after = jnp.where(col == cols - 1, 0.0, pltpu.roll(wide, cols - 1, 0)).astype(BF16)
    base = at * 3 * chans
    taps[:, base : base + chans] = before
    taps[:, base + chans : base + 2 * chans] = x
    taps[:, base + 2 * chans : base + 3 * chans] = after


def in_hbm(*arrays):
    return [pltpu.with_memory_space_constraint(x, HBM) for x in arrays]


def in_vmem(x):
    return pltpu.with_memory_space_constraint(x, VMEM)


def odd_device():
    return lax.rem(lax.axis_index("sp"), 2)


def edge_terms(taps, w, o_ref):
    clips, cols, wide = taps.shape
    ch = w.shape[1]

    def term(f, low, high):
        return dot(
            taps[:, :, f * 3 * ch : (f + 1) * 3 * ch].reshape(clips * cols, 3 * ch),
            w[:, :, low * ch : high * ch].reshape(3 * ch, (high - low) * ch),
        )

    both = term(1, 1, 3) + term(2, 0, 2)
    first = both[:, :ch] + term(0, 2, 3)
    last = both[:, ch:] + term(3, 0, 1)
    for c in range(clips):
        rows = slice(c * cols, (c + 1) * cols)
        o_ref[c, 0] = first[rows].astype(BF16)
        o_ref[c, 1] = last[rows].astype(BF16)


def edge_sums(frames, weight, projection):
    clips, depth, rows, cols, ch = frames.shape
    latents = projection.shape[0]

    def kernel(
        x_hbm, w_hbm, p_hbm, near_ref, far_ref, near_taps, far_taps, inner, placed, x, w, p, x_sem, w_sem, i_sem, p_sem
    ):
        odd = odd_device()
        in_p = pltpu.make_async_copy(p_hbm, p, p_sem)
        in_x, in_w = [], []
        for e, (row, tap) in enumerate(((1 - odd, 2 * odd), (odd, 2 - 2 * odd))):
            in_x.append(
                [pltpu.make_async_copy(x_hbm.at[c, :, row], x.at[e, c], x_sem.at[e, c]) for c in range(clips)]
            )
            in_w.append(
                [
                    pltpu.make_async_copy(w_hbm.at[a, tap], w.at[e, :, :, pl.ds((2 - a) * ch, ch)], w_sem.at[e, a])
                    for a in range(3)
                ]
            )
        in_inner = [
            pltpu.make_async_copy(w_hbm.at[a, b], inner.at[a, :, :, pl.ds(place * ch, ch)], i_sem.at[a, place])
            for a in range(3)
            for place, b in enumerate((2 * odd, 1, 2 - 2 * odd))
        ]
        in_x[0][0].start()
        for copy in in_w[0]:
            copy.start()
        in_x[0][1].start()
        in_p.start()
        in_x[0][0].wait()
        for f in range(depth):
            spread_taps(x[0, 0, f], near_taps.at[0], f)
        in_p.wait()
        k = lax.broadcasted_iota(jnp.int32, (latents, 128), 0)
        lane = lax.broadcasted_iota(jnp.int32, (latents, 128), 1)
        for c in range(clips):
            for t in range(2):
                pick = (lane % 64 == t * 32 + c * latents + k).astype(F32).astype(BF16)
                turned = lax.dot_general(p[...], pick, (((0,), (0,)), ((), ())), preferred_element_type=F32)
                at = (c * 2 + t) * ch
                placed[at : at + ch] = turned.astype(BF16)
        for copy in in_w[0]:
            copy.wait()
        for copy in in_x[1] + in_w[1]:
            copy.start()
        edge_terms(near_taps.at[0:1], w.at[0], near_ref.at[0:1])
        in_x[0][1].wait()
        for f in range(depth):
            spread_taps(x[0, 1, f], near_taps.at[1], f)
        edge_terms(near_taps.at[1:2], w.at[0], near_ref.at[1:2])
        for copy in in_inner:
            copy.start()
        for copy in in_w[1]:
            copy.wait()
        for c in range(clips):
            in_x[1][c].wait()
            for f in range(depth):
                spread_taps(x[1, c, f], far_taps.at[c], f)
            edge_terms(far_taps.at[c : c + 1], w.at[1], far_ref.at[c : c + 1])
        for copy in in_inner:
            copy.wait()

    edge = jax.ShapeDtypeStruct((clips, 2, cols, ch), BF16)
    taps = pltpu.VMEM((clips, cols, depth * 3 * ch), BF16)
    return pl.pallas_call(
        kernel,
        in_specs=[IN_HBM] * 3,
        out_specs=[IN_VMEM] * 6,
        out_shape=[edge, edge, taps, taps, pltpu.VMEM((3, 3, ch, 3 * ch), BF16), pltpu.VMEM((4 * ch, 128), BF16)],
        scratch_shapes=[
            pltpu.VMEM((rows, clips, depth, cols, ch), BF16),
            pltpu.VMEM((rows, 3, ch, 3 * ch), BF16),
            pltpu.VMEM((latents, ch), BF16),
            DMA((rows, clips)),
            DMA((rows, 3)),
            DMA((3, 3)),
            DMA,
        ],
        compiler_params=params(20),
        cost_estimate=cost(clips * 4 * cols * 9 * ch * ch, 16 * 10**6),
    )(*in_hbm(frames, weight, projection))


def inner_sums(near, far, weight):
    clips, cols, _ = near.shape
    ch = weight.shape[2]

    def kernel(near, far, w, out):
        for c in range(clips):
            for t in range(2):
                window = slice(t * 3 * ch, (t + 3) * 3 * ch)
                out[c, t] = dot(near[c, :, window], w[:, :, :, ch:].reshape(9 * ch, 2 * ch)) + dot(
                    far[c, :, window], w[:, :, :, : 2 * ch].reshape(9 * ch, 2 * ch)
                )

    return pl.pallas_call(
        kernel,
        in_specs=[IN_VMEM] * 3,
        out_specs=IN_VMEM,
        out_shape=pltpu.VMEM((clips, 2, cols, 2 * ch), F32),
        compiler_params=params(16),
        cost_estimate=cost(clips * 8 * cols * 9 * ch * ch, 14 * 10**6),
    )(near, far, weight)


def row_latents(sums, part, halo, bias, placed, before=None):
    clips, outs, cols, wide = sums.shape
    ch = wide // 2
    lanes = placed.shape[1]

    def over_channels(x, pick):
        x = pick(x, pltpu.roll(x, lanes // 8, 1))
        return pick(x, pltpu.roll(x, lanes // 4, 1))

    def kernel(s_ref, halo_ref, b_ref, p_ref, *refs):
        o_ref, ends_ref, hidden = refs[-3:]
        for c in range(clips):
            for t in range(outs):
                v = s_ref[c, t, :, part * ch : (part + 1) * ch] + halo_ref[c, t].astype(F32) + b_ref[...]
                v = v * 0.5
                at = (c * outs + t) * ch
                hidden[:, at : at + ch] = (v + v * jnp.tanh(v)).astype(BF16)
        found = dot(hidden[...], p_ref[...])
        o_ref[:cols] = found
        o_ref[cols:] = jnp.zeros_like(o_ref[cols:])
        low = over_channels(jnp.min(found, axis=0, keepdims=True), jnp.minimum)
        high = over_channels(jnp.max(found, axis=0, keepdims=True), jnp.maximum)
        first = lax.broadcasted_iota(jnp.int32, (8, lanes), 0) == 0
        if before is None:
            ends_ref[...] = jnp.where(first, low, high)
        else:
            ends_ref[...] = jnp.where(first, jnp.minimum(low, refs[0][...]), jnp.maximum(high, refs[0][...]))

    args = [sums, halo, bias, placed] + ([] if before is None else [before])
    return pl.pallas_call(
        kernel,
        in_specs=[IN_VMEM] * len(args),
        out_specs=[IN_VMEM] * 2,
        out_shape=[pltpu.VMEM((cols + 8, lanes), F32), pltpu.VMEM((8, lanes), F32)],
        scratch_shapes=[pltpu.VMEM((cols, clips * outs * ch), BF16)],
        compiler_params=params(16),
        cost_estimate=cost(cols * clips * outs * ch * lanes, 2 * 10**6),
    )(*args)


def latent_messages(near, far, ends, other_ends, shards, copies):
    padded, lanes = near.shape
    half = lanes // 2
    share = (padded - 8) // shards

    def in_terms(x):
        first = x.astype(BF16).astype(F32)
        second = (x - first).astype(BF16).astype(F32)
        third = x - first - second
        block = lax.broadcasted_iota(jnp.int32, x.shape, 1) // (half // 4)
        return jnp.where(block == 4, first, jnp.where(block == 5, second, jnp.where(block == 6, third, 0.0)))

    def kernel(near_ref, far_ref, e_ref, other_ref, o_ref, latent):
        odd = odd_device()
        latent[1 - odd] = near_ref[...]
        latent[odd] = far_ref[...]
        lowest = jnp.minimum(e_ref[0:1], other_ref[0:1])
        highest = jnp.maximum(e_ref[1:2], other_ref[1:2])
        middle = (lowest + highest) * 0.5
        at_end = (lax.broadcasted_iota(jnp.int32, (8, lanes), 0) == 7) & (
            lax.broadcasted_iota(jnp.int32, (8, lanes), 1) >= half
        )
        in_front = lax.broadcasted_iota(jnp.int32, (8, lanes), 1) < half
        ends = (in_terms(lowest), in_terms(highest))
        for s in range(shards):
            rows = []
            for r in range(2):
                first = latent[r, pl.ds(share * s, 8)]
                second = latent[r, pl.ds(share * s + 8, 8)]
                rows.append(jnp.where(at_end, ends[r], jnp.where(in_front, first, second) - middle))
            message = jnp.concatenate(rows, axis=0).astype(BF16)
            for g in range(copies):
                o_ref[g, s] = message

    return pl.pallas_call(
        kernel,
        in_specs=[IN_VMEM] * 4,
        out_specs=IN_VMEM,
        out_shape=pltpu.VMEM((copies, shards, 16, lanes), BF16),
        scratch_shapes=[pltpu.VMEM((2, padded, lanes), F32)],
        compiler_params=params(16),
    )(near, far, ends, other_ends)


def coded_columns(received, share):
    groups, shards, _, lanes = received.shape
    latents = lanes // 8
    channels = lanes // 4

    def kernel(x_ref, o_ref, coded, turned):
        block = lax.broadcasted_iota(jnp.int32, (1, lanes), 1) // latents

        def end(g, row):
            terms = x_ref[g].astype(F32)[:, row, :]
            return terms + pltpu.roll(terms, lanes - latents, 1) + pltpu.roll(terms, lanes - 2 * latents, 1)

        def to_all(x):
            x = jnp.where(block == 4, x, 0.0)
            for step in (1, 2, 4):
                x = x + pltpu.roll(x, step * latents, 1)
            return x

        lows = [end(g, 7) for g in range(groups)]
        highs = [end(g, 15) for g in range(groups)]
        low = jnp.min(functools.reduce(jnp.minimum, lows), axis=0, keepdims=True)
        high = jnp.max(functools.reduce(jnp.maximum, highs), axis=0, keepdims=True)
        low, high = to_all(low), to_all(high)
        mine = lax.div(lax.axis_index("grp"), 2)
        middle = to_all((end(mine, 7) + end(mine, 15)) * 0.5)
        x = x_ref[mine].astype(F32) + middle[:, None, :]
        coded[...] = ((x - low) / (high - low) * 2.0 - 1.0).reshape(shards * 16, lanes)
        for first in range(8):
            piece_of = coded[pl.ds(first, 2 * shards, stride=8), :].T
            for piece in range(4):
                w, t = first + 8 * (piece // 2), piece % 2
                if w < share:
                    rows = piece_of[piece * channels : (piece + 1) * channels]
                    turned[pl.ds(2 * w + t, channels, stride=2 * share), :] = rows
        o_ref[...] = turned[...].astype(BF16)

    return pl.pallas_call(
        kernel,
        in_specs=[IN_VMEM],
        out_specs=IN_VMEM,
        out_shape=jax.ShapeDtypeStruct((channels * share * 2, 2 * shards), BF16),
        scratch_shapes=[pltpu.VMEM((shards * 16, lanes), F32), pltpu.VMEM((channels * share * 2, 2 * shards), F32)],
        compiler_params=params(16),
    )(in_vmem(received))


def on_device(frames, conv_weight, conv_bias, projection):
    clips, depth, rows, cols, ch = frames.shape
    latents = projection.shape[1]
    outs = depth - 2
    shards, groups = lax.axis_size("sp"), lax.axis_size("grp")
    share = cols // shards

    def swap(x, first):
        pairs = [(i, i + 1) for i in range(first, shards - 1, 2)]
        return lax.ppermute(x, "sp", pairs + [(b, a) for a, b in pairs])

    near_sums, far_sums, near_taps, far_taps, inner_w, placed = edge_sums(frames, conv_weight, projection.T)
    near, far = swap(near_sums, 0), swap(far_sums, 1)
    sums = inner_sums(near_taps, far_taps, inner_w)

    bias = conv_bias.reshape(1, ch)
    near_latents, near_ends = row_latents(sums, 0, near, bias, placed)
    far_latents, ends = row_latents(sums, 1, far, bias, placed, near_ends)
    other_ends = lax.ppermute(ends, "grp", [(i, i ^ 1) for i in range(groups)])
    messages = latent_messages(near_latents, far_latents, ends, other_ends, shards, groups // 2)
    messages = messages.reshape(groups // 2 * shards, 16, messages.shape[-1])
    same_core = [[(2 * y + core) * shards + s for y in range(groups // 2) for s in range(shards)] for core in range(2)]
    received = lax.all_to_all(messages, ("grp", "sp"), 0, 0, axis_index_groups=same_core)
    coded = coded_columns(received.reshape(groups // 2, shards, 16, -1), share)
    return coded.reshape(clips, latents, share, outs, rows * shards).transpose(0, 1, 3, 2, 4)


def solution(mesh):
    placed = (P("grp", None, "sp", None, None), P(), P(), P())
    return jax.shard_map(
        on_device,
        mesh=mesh,
        in_specs=placed,
        out_specs=P("grp", None, None, "sp", None),
        check_vma=False,
    )
```

```python
import functools

import jax
import jax.numpy as jnp
from jax import lax
from jax.experimental import pallas as pl
from jax.experimental.pallas import tpu as pltpu
from jax.sharding import PartitionSpec as P

F32, BF16 = jnp.float32, jnp.bfloat16
HBM, VMEM = pltpu.MemorySpace.HBM, pltpu.MemorySpace.VMEM
IN_HBM, IN_VMEM = pl.BlockSpec(memory_space=HBM), pl.BlockSpec(memory_space=VMEM)
DMA = pltpu.SemaphoreType.DMA


def dot(a, b):
    return jnp.dot(a, b, preferred_element_type=F32)


def cost(macs, nbytes):
    return pl.CostEstimate(flops=2 * macs, bytes_accessed=nbytes, transcendentals=0)


def params(mib):
    return pltpu.CompilerParams(vmem_limit_bytes=mib * 2**20)


def spread_taps(x, taps, at):
    cols, chans = x.shape
    wide = x.astype(F32)
    col = lax.broadcasted_iota(jnp.int32, wide.shape, 0)
    before = jnp.where(col == 0, 0.0, pltpu.roll(wide, 1, 0)).astype(BF16)
    after = jnp.where(col == cols - 1, 0.0, pltpu.roll(wide, cols - 1, 0)).astype(BF16)
    base = at * 3 * chans
    taps[:, base : base + chans] = before
    taps[:, base + chans : base + 2 * chans] = x
    taps[:, base + 2 * chans : base + 3 * chans] = after


def in_hbm(*arrays):
    return [pltpu.with_memory_space_constraint(x, HBM) for x in arrays]


def in_vmem(x):
    return pltpu.with_memory_space_constraint(x, VMEM)


def odd_device():
    return lax.rem(lax.axis_index("sp"), 2)


def edge_terms(taps, w, o_ref):
    ch = w.shape[1]

    def term(f, low, high):
        return dot(
            taps[:, f * 3 * ch : (f + 1) * 3 * ch],
            w[:, :, low * ch : high * ch].reshape(3 * ch, (high - low) * ch),
        )

    both = term(1, 1, 3) + term(2, 0, 2)
    o_ref[0] = (both[:, :ch] + term(0, 2, 3)).astype(BF16)
    o_ref[1] = (both[:, ch:] + term(3, 0, 1)).astype(BF16)


def first_edges(frames, weight, projection):
    clips, depth, _, cols, ch = frames.shape
    latents = projection.shape[0]

    def kernel(
        x_hbm, w_hbm, p_hbm, near_ref, far_ref, near_taps, far_taps, x1, far_w, inner, placed,
        x, w, p, x_sem, w_sem, i_sem, p_sem,
    ):
        odd = odd_device()
        in_p = pltpu.make_async_copy(p_hbm, p, p_sem)
        in_near = [pltpu.make_async_copy(x_hbm.at[c, :, 1 - odd], x.at[c], x_sem.at[c]) for c in range(clips)]
        in_far = pltpu.make_async_copy(x_hbm.at[0, :, odd], x.at[2], x_sem.at[2])
        in_far1 = pltpu.make_async_copy(x_hbm.at[1, :, odd], x1, x_sem.at[3])
        in_w, in_far_w = (
            [
                pltpu.make_async_copy(w_hbm.at[a, tap], to.at[:, :, pl.ds((2 - a) * ch, ch)], w_sem.at[e, a])
                for a in range(3)
            ]
            for e, (tap, to) in enumerate(((2 * odd, w), (2 - 2 * odd, far_w)))
        )
        in_inner = [
            pltpu.make_async_copy(w_hbm.at[a, b], inner.at[a, :, :, pl.ds(place * ch, ch)], i_sem.at[a, place])
            for a in range(3)
            for place, b in enumerate((2 * odd, 1, 2 - 2 * odd))
        ]
        in_near[0].start()
        for copy in in_w:
            copy.start()
        in_near[1].start()
        in_p.start()
        in_near[0].wait()
        for f in range(depth):
            spread_taps(x[0, f], near_taps.at[0], f)
        in_p.wait()
        k = lax.broadcasted_iota(jnp.int32, (latents, 128), 0)
        lane = lax.broadcasted_iota(jnp.int32, (latents, 128), 1)
        for c in range(clips):
            for t in range(2):
                pick = (lane % 64 == t * 32 + c * latents + k).astype(F32).astype(BF16)
                turned = lax.dot_general(p[...], pick, (((0,), (0,)), ((), ())), preferred_element_type=F32)
                at = (c * 2 + t) * ch
                placed[at : at + ch] = turned.astype(BF16)
        for copy in in_w:
            copy.wait()
        for copy in [in_far, *in_far_w, in_far1]:
            copy.start()
        edge_terms(near_taps.at[0], w, near_ref.at[0])
        in_near[1].wait()
        for f in range(depth):
            spread_taps(x[1, f], near_taps.at[1], f)
        for copy in in_inner:
            copy.start()
        edge_terms(near_taps.at[1], w, near_ref.at[1])
        in_far.wait()
        for f in range(depth):
            spread_taps(x[2, f], far_taps, f)
        for copy in in_far_w:
            copy.wait()
        edge_terms(far_taps, far_w, far_ref)
        for copy in [in_far1, *in_inner]:
            copy.wait()

    return pl.pallas_call(
        kernel,
        in_specs=[IN_HBM] * 3,
        out_specs=[IN_VMEM] * 8,
        out_shape=[
            pltpu.VMEM((clips, 2, cols, ch), BF16),
            pltpu.VMEM((2, cols, ch), BF16),
            pltpu.VMEM((clips, cols, depth * 3 * ch), BF16),
            pltpu.VMEM((cols, depth * 3 * ch), BF16),
            pltpu.VMEM((depth, cols, ch), BF16),
            pltpu.VMEM((3, ch, 3 * ch), BF16),
            pltpu.VMEM((3, 3, ch, 3 * ch), BF16),
            pltpu.VMEM((clips * 2 * ch, 128), BF16),
        ],
        scratch_shapes=[
            pltpu.VMEM((3, depth, cols, ch), BF16),
            pltpu.VMEM((3, ch, 3 * ch), BF16),
            pltpu.VMEM((latents, ch), BF16),
            DMA((4,)),
            DMA((2, 3)),
            DMA((3, 3)),
            DMA,
        ],
        compiler_params=params(16),
    )(*in_hbm(frames, weight, projection))


def last_edges(x1, edge_w):
    depth, cols, ch = x1.shape

    def kernel(x, w, o_ref, taps):
        for f in range(depth):
            spread_taps(x[f], taps, f)
        edge_terms(taps, w, o_ref)

    return pl.pallas_call(
        kernel,
        in_specs=[IN_VMEM] * 2,
        out_specs=[IN_VMEM] * 2,
        out_shape=[pltpu.VMEM((2, cols, ch), BF16), pltpu.VMEM((cols, depth * 3 * ch), BF16)],
        compiler_params=params(16),
    )(x1, edge_w)


def inner_sums(near, far, weight):
    clips, cols, _ = near.shape
    ch = weight.shape[2]

    def kernel(near, far0, far1, w, out):
        for c, far in enumerate((far0, far1)):
            for t in range(2):
                window = slice(t * 3 * ch, (t + 3) * 3 * ch)
                out[c, t] = dot(near[c, :, window], w[:, :, :, ch:].reshape(9 * ch, 2 * ch)) + dot(
                    far[:, window], w[:, :, :, : 2 * ch].reshape(9 * ch, 2 * ch)
                )

    return pl.pallas_call(
        kernel,
        in_specs=[IN_VMEM] * 4,
        out_specs=IN_VMEM,
        out_shape=pltpu.VMEM((clips, 2, cols, 2 * ch), F32),
        compiler_params=params(16),
    )(near, *far, weight)


def over_channels(x, pick):
    lanes = x.shape[1]
    x = pick(x, pltpu.roll(x, lanes // 8, 1))
    return pick(x, pltpu.roll(x, lanes // 4, 1))


def hidden_units(sums, halo, bias):
    h = (sums + halo.astype(F32) + bias) * 0.5
    return (h + h * jnp.tanh(h)).astype(BF16)


def first_latents(sums, near, far0, bias, placed):
    clips, outs, cols, wide = sums.shape
    ch = wide // 2
    lanes = placed.shape[1]

    def kernel(s_ref, near_ref, far0_ref, b_ref, p_ref, near_out, far_out, ends_ref, hidden):
        for c in range(clips):
            for t in range(outs):
                at = (c * outs + t) * ch
                hidden[0, :, at : at + ch] = hidden_units(s_ref[c, t, :, :ch], near_ref[c, t], b_ref[...])
        for t in range(outs):
            hidden[1, :, t * ch : (t + 1) * ch] = hidden_units(s_ref[0, t, :, ch:], far0_ref[t], b_ref[...])
        found = dot(hidden[0], p_ref[...])
        near_out[:cols] = found
        near_out[cols:] = jnp.zeros_like(near_out[cols:])
        far_out[...] = dot(hidden[1, :, : outs * ch], p_ref[: outs * ch])
        low = over_channels(jnp.min(found, axis=0, keepdims=True), jnp.minimum)
        high = over_channels(jnp.max(found, axis=0, keepdims=True), jnp.maximum)
        ends_ref[...] = jnp.where(lax.broadcasted_iota(jnp.int32, (8, lanes), 0) == 0, low, high)

    return pl.pallas_call(
        kernel,
        in_specs=[IN_VMEM] * 5,
        out_specs=[IN_VMEM] * 3,
        out_shape=[pltpu.VMEM((cols + 8, lanes), F32), pltpu.VMEM((cols, lanes), F32), pltpu.VMEM((8, lanes), F32)],
        scratch_shapes=[pltpu.VMEM((2, cols, clips * outs * ch), BF16)],
        compiler_params=params(16),
    )(sums, near, far0, bias, placed)


def last_latents(sums, far1, bias, placed, far_latents0, near_ends):
    clips, outs, cols, wide = sums.shape
    ch = wide // 2
    lanes = placed.shape[1]

    def kernel(s_ref, far1_ref, b_ref, p_ref, far0_ref, near_ref, far_out, ends_ref, hidden):
        for t in range(outs):
            hidden[:, t * ch : (t + 1) * ch] = hidden_units(s_ref[1, t, :, ch:], far1_ref[t], b_ref[...])
        found = dot(hidden[...], p_ref[outs * ch :]) + far0_ref[...]
        far_out[:cols] = found
        far_out[cols:] = jnp.zeros_like(far_out[cols:])
        low = jnp.minimum(over_channels(jnp.min(found, axis=0, keepdims=True), jnp.minimum), near_ref[...])
        high = jnp.maximum(over_channels(jnp.max(found, axis=0, keepdims=True), jnp.maximum), near_ref[...])
        ends_ref[...] = jnp.where(lax.broadcasted_iota(jnp.int32, (8, lanes), 0) == 0, low, high)

    return pl.pallas_call(
        kernel,
        in_specs=[IN_VMEM] * 6,
        out_specs=[IN_VMEM] * 2,
        out_shape=[pltpu.VMEM((cols + 8, lanes), F32), pltpu.VMEM((8, lanes), F32)],
        scratch_shapes=[pltpu.VMEM((cols, outs * ch), BF16)],
        compiler_params=params(16),
    )(sums, far1, bias, placed, far_latents0, near_ends)


def latent_messages(near, far, ends, other_ends, shards, copies):
    padded, lanes = near.shape
    half = lanes // 2
    share = (padded - 8) // shards

    def in_terms(x):
        first = x.astype(BF16).astype(F32)
        second = (x - first).astype(BF16).astype(F32)
        third = x - first - second
        block = lax.broadcasted_iota(jnp.int32, x.shape, 1) // (half // 4)
        return jnp.where(block == 4, first, jnp.where(block == 5, second, jnp.where(block == 6, third, 0.0)))

    def kernel(near_ref, far_ref, e_ref, other_ref, o_ref, latent):
        odd = odd_device()
        latent[1 - odd] = near_ref[...]
        latent[odd] = far_ref[...]
        lowest = jnp.minimum(e_ref[0:1], other_ref[0:1])
        highest = jnp.maximum(e_ref[1:2], other_ref[1:2])
        middle = (lowest + highest) * 0.5
        at_end = (lax.broadcasted_iota(jnp.int32, (8, lanes), 0) == 7) & (
            lax.broadcasted_iota(jnp.int32, (8, lanes), 1) >= half
        )
        in_front = lax.broadcasted_iota(jnp.int32, (8, lanes), 1) < half
        ends = (in_terms(lowest), in_terms(highest))
        for s in range(shards):
            rows = []
            for r in range(2):
                first = latent[r, pl.ds(share * s, 8)]
                second = latent[r, pl.ds(share * s + 8, 8)]
                rows.append(jnp.where(at_end, ends[r], jnp.where(in_front, first, second) - middle))
            message = jnp.concatenate(rows, axis=0).astype(BF16)
            for g in range(copies):
                o_ref[g, s] = message

    return pl.pallas_call(
        kernel,
        in_specs=[IN_VMEM] * 4,
        out_specs=IN_VMEM,
        out_shape=pltpu.VMEM((copies, shards, 16, lanes), BF16),
        scratch_shapes=[pltpu.VMEM((2, padded, lanes), F32)],
        compiler_params=params(16),
    )(near, far, ends, other_ends)


def coded_columns(received, share):
    groups, shards, _, lanes = received.shape
    latents = lanes // 8
    channels = lanes // 4

    def kernel(x_ref, o_ref, coded, turned):
        block = lax.broadcasted_iota(jnp.int32, (1, lanes), 1) // latents

        def end(g, row):
            terms = x_ref[g].astype(F32)[:, row, :]
            return terms + pltpu.roll(terms, lanes - latents, 1) + pltpu.roll(terms, lanes - 2 * latents, 1)

        def to_all(x):
            x = jnp.where(block == 4, x, 0.0)
            for step in (1, 2, 4):
                x = x + pltpu.roll(x, step * latents, 1)
            return x

        lows = [end(g, 7) for g in range(groups)]
        highs = [end(g, 15) for g in range(groups)]
        low = jnp.min(functools.reduce(jnp.minimum, lows), axis=0, keepdims=True)
        high = jnp.max(functools.reduce(jnp.maximum, highs), axis=0, keepdims=True)
        low, high = to_all(low), to_all(high)
        mine = lax.div(lax.axis_index("grp"), 2)
        middle = to_all((end(mine, 7) + end(mine, 15)) * 0.5)
        x = x_ref[mine].astype(F32) + middle[:, None, :]
        coded[...] = ((x - low) / (high - low) * 2.0 - 1.0).reshape(shards * 16, lanes)
        for first in range(8):
            piece_of = coded[pl.ds(first, 2 * shards, stride=8), :].T
            for piece in range(4):
                w, t = first + 8 * (piece // 2), piece % 2
                if w < share:
                    rows = piece_of[piece * channels : (piece + 1) * channels]
                    turned[pl.ds(2 * w + t, channels, stride=2 * share), :] = rows
        o_ref[...] = turned[...].astype(BF16)

    return pl.pallas_call(
        kernel,
        in_specs=[IN_VMEM],
        out_specs=IN_VMEM,
        out_shape=jax.ShapeDtypeStruct((channels * share * 2, 2 * shards), BF16),
        scratch_shapes=[pltpu.VMEM((shards * 16, lanes), F32), pltpu.VMEM((channels * share * 2, 2 * shards), F32)],
        compiler_params=params(16),
    )(in_vmem(received))


def on_device(frames, conv_weight, conv_bias, projection):
    clips, depth, rows, cols, ch = frames.shape
    latents = projection.shape[1]
    outs = depth - 2
    shards, groups = lax.axis_size("sp"), lax.axis_size("grp")
    share = cols // shards

    def swap(x, first):
        pairs = [(i, i + 1) for i in range(first, shards - 1, 2)]
        return lax.ppermute(x, "sp", pairs + [(b, a) for a, b in pairs])

    near_sums, far_sums0, near_taps, far_taps0, x1, far_w, inner, placed = first_edges(frames, conv_weight, projection.T)
    near, far0 = swap(near_sums, 0), swap(far_sums0, 1)
    far_sums1, far_taps1 = last_edges(x1, far_w)
    far1 = swap(far_sums1, 1)
    sums = inner_sums(near_taps, (far_taps0, far_taps1), inner)

    bias = conv_bias.reshape(1, ch)
    near_latents, far_latents0, near_ends = first_latents(sums, near, far0, bias, placed)
    far_latents, ends = last_latents(sums, far1, bias, placed, far_latents0, near_ends)
    other_ends = lax.ppermute(ends, "grp", [(i, i ^ 1) for i in range(groups)])
    messages = latent_messages(near_latents, far_latents, ends, other_ends, shards, groups // 2)
    messages = messages.reshape(groups // 2 * shards, 16, messages.shape[-1])
    same_core = [[(2 * y + core) * shards + s for y in range(groups // 2) for s in range(shards)] for core in range(2)]
    received = lax.all_to_all(messages, ("grp", "sp"), 0, 0, axis_index_groups=same_core)
    coded = coded_columns(received.reshape(groups // 2, shards, 16, -1), share)
    return coded.reshape(clips, latents, share, outs, rows * shards).transpose(0, 1, 3, 2, 4)


def solution(mesh):
    placed = (P("grp", None, "sp", None, None), P(), P(), P())
    return jax.shard_map(
        on_device,
        mesh=mesh,
        in_specs=placed,
        out_specs=P("grp", None, None, "sp", None),
        check_vma=False,
    )
```

```python
import functools

import jax
import jax.numpy as jnp
from jax import lax
from jax.experimental import pallas as pl
from jax.experimental.pallas import tpu as pltpu
from jax.sharding import PartitionSpec as P

F32, BF16 = jnp.float32, jnp.bfloat16
HBM, VMEM = pltpu.MemorySpace.HBM, pltpu.MemorySpace.VMEM
IN_HBM, IN_VMEM = pl.BlockSpec(memory_space=HBM), pl.BlockSpec(memory_space=VMEM)
DMA = pltpu.SemaphoreType.DMA


def dot(a, b):
    return jnp.dot(a, b, preferred_element_type=F32)


def cost(macs, nbytes):
    return pl.CostEstimate(flops=2 * macs, bytes_accessed=nbytes, transcendentals=0)


def params(mib):
    return pltpu.CompilerParams(vmem_limit_bytes=mib * 2**20)


def spread_taps(x, taps, at):
    cols, chans = x.shape
    wide = x.astype(F32)
    col = lax.broadcasted_iota(jnp.int32, wide.shape, 0)
    before = jnp.where(col == 0, 0.0, pltpu.roll(wide, 1, 0)).astype(BF16)
    after = jnp.where(col == cols - 1, 0.0, pltpu.roll(wide, cols - 1, 0)).astype(BF16)
    base = at * 3 * chans
    taps[:, base : base + chans] = before
    taps[:, base + chans : base + 2 * chans] = x
    taps[:, base + 2 * chans : base + 3 * chans] = after


def in_hbm(*arrays):
    return [pltpu.with_memory_space_constraint(x, HBM) for x in arrays]


def in_vmem(x):
    return pltpu.with_memory_space_constraint(x, VMEM)


def odd_device():
    return lax.rem(lax.axis_index("sp"), 2)


def edge_terms(taps, w, o_ref):
    ch = w.shape[1]

    def term(f, low, high):
        return dot(
            taps[:, f * 3 * ch : (f + 1) * 3 * ch],
            w[:, :, low * ch : high * ch].reshape(3 * ch, (high - low) * ch),
        )

    both = term(1, 1, 3) + term(2, 0, 2)
    o_ref[0] = (both[:, :ch] + term(0, 2, 3)).astype(BF16)
    o_ref[1] = (both[:, ch:] + term(3, 0, 1)).astype(BF16)


def first_edges(frames, weight, projection):
    clips, depth, _, cols, ch = frames.shape
    latents = projection.shape[0]

    def kernel(
        x_hbm, w_hbm, p_hbm, near_ref, far_ref, near_taps, far_taps, x1, far_w, inner, placed,
        x, w, p, x_sem, w_sem, i_sem, p_sem,
    ):
        odd = odd_device()
        in_p = pltpu.make_async_copy(p_hbm, p, p_sem)
        in_near = [pltpu.make_async_copy(x_hbm.at[c, :, 1 - odd], x.at[c], x_sem.at[c]) for c in range(clips)]
        in_far = pltpu.make_async_copy(x_hbm.at[0, :, odd], x.at[2], x_sem.at[2])
        in_far1 = pltpu.make_async_copy(x_hbm.at[1, :, odd], x1, x_sem.at[3])
        in_w, in_far_w = (
            [
                pltpu.make_async_copy(w_hbm.at[a, tap], to.at[:, :, pl.ds((2 - a) * ch, ch)], w_sem.at[e, a])
                for a in range(3)
            ]
            for e, (tap, to) in enumerate(((2 * odd, w), (2 - 2 * odd, far_w)))
        )
        in_inner = [
            pltpu.make_async_copy(w_hbm.at[a, b], inner.at[a, :, :, pl.ds(place * ch, ch)], i_sem.at[a, place])
            for a in range(3)
            for place, b in enumerate((2 * odd, 1, 2 - 2 * odd))
        ]
        in_near[0].start()
        for copy in in_w:
            copy.start()
        in_near[1].start()
        in_p.start()
        in_near[0].wait()
        for f in range(depth):
            spread_taps(x[0, f], near_taps.at[0], f)
        in_p.wait()
        k = lax.broadcasted_iota(jnp.int32, (latents, 128), 0)
        lane = lax.broadcasted_iota(jnp.int32, (latents, 128), 1)
        for c in range(clips):
            for t in range(2):
                pick = (lane % 64 == t * 32 + c * latents + k).astype(F32).astype(BF16)
                turned = lax.dot_general(p[...], pick, (((0,), (0,)), ((), ())), preferred_element_type=F32)
                at = (c * 2 + t) * ch
                placed[at : at + ch] = turned.astype(BF16)
        for copy in in_w:
            copy.wait()
        for copy in [in_far, *in_far_w, in_far1]:
            copy.start()
        edge_terms(near_taps.at[0], w, near_ref.at[0])
        in_near[1].wait()
        for f in range(depth):
            spread_taps(x[1, f], near_taps.at[1], f)
        for copy in in_inner:
            copy.start()
        edge_terms(near_taps.at[1], w, near_ref.at[1])
        in_far.wait()
        for f in range(depth):
            spread_taps(x[2, f], far_taps, f)
        for copy in in_far_w:
            copy.wait()
        edge_terms(far_taps, far_w, far_ref)
        for copy in [in_far1, *in_inner]:
            copy.wait()

    return pl.pallas_call(
        kernel,
        in_specs=[IN_HBM] * 3,
        out_specs=[IN_VMEM] * 8,
        out_shape=[
            pltpu.VMEM((clips, 2, cols, ch), BF16),
            pltpu.VMEM((2, cols, ch), BF16),
            pltpu.VMEM((clips, cols, depth * 3 * ch), BF16),
            pltpu.VMEM((cols, depth * 3 * ch), BF16),
            pltpu.VMEM((depth, cols, ch), BF16),
            pltpu.VMEM((3, ch, 3 * ch), BF16),
            pltpu.VMEM((3, 3, ch, 3 * ch), BF16),
            pltpu.VMEM((clips * 2 * ch, 128), BF16),
        ],
        scratch_shapes=[
            pltpu.VMEM((3, depth, cols, ch), BF16),
            pltpu.VMEM((3, ch, 3 * ch), BF16),
            pltpu.VMEM((latents, ch), BF16),
            DMA((4,)),
            DMA((2, 3)),
            DMA((3, 3)),
            DMA,
        ],
        compiler_params=params(16),
    )(*in_hbm(frames, weight, projection))


def last_edges(x1, edge_w):
    depth, cols, ch = x1.shape

    def kernel(x, w, o_ref, taps):
        for f in range(depth):
            spread_taps(x[f], taps, f)
        edge_terms(taps, w, o_ref)

    return pl.pallas_call(
        kernel,
        in_specs=[IN_VMEM] * 2,
        out_specs=[IN_VMEM] * 2,
        out_shape=[pltpu.VMEM((2, cols, ch), BF16), pltpu.VMEM((cols, depth * 3 * ch), BF16)],
        compiler_params=params(16),
    )(x1, edge_w)


def inner_sums(near, far, weight):
    clips, cols, _ = near.shape
    ch = weight.shape[2]

    def kernel(near, far0, far1, w, out):
        for c, far in enumerate((far0, far1)):
            for t in range(2):
                window = slice(t * 3 * ch, (t + 3) * 3 * ch)
                out[c, t] = dot(near[c, :, window], w[:, :, :, ch:].reshape(9 * ch, 2 * ch)) + dot(
                    far[:, window], w[:, :, :, : 2 * ch].reshape(9 * ch, 2 * ch)
                )

    return pl.pallas_call(
        kernel,
        in_specs=[IN_VMEM] * 4,
        out_specs=IN_VMEM,
        out_shape=pltpu.VMEM((clips, 2, cols, 2 * ch), F32),
        compiler_params=params(16),
    )(near, *far, weight)


def over_channels(x, pick):
    lanes = x.shape[1]
    x = pick(x, pltpu.roll(x, lanes // 8, 1))
    return pick(x, pltpu.roll(x, lanes // 4, 1))


def hidden_units(sums, halo, bias):
    h = (sums + halo.astype(F32) + bias) * 0.5
    return (h + h * jnp.tanh(h)).astype(BF16)


def arrival(halo):
    def kernel(x_ref, o_ref):
        o_ref[...] = x_ref[0, :16, :128].astype(F32)

    return pl.pallas_call(
        kernel,
        in_specs=[IN_VMEM],
        out_specs=IN_VMEM,
        out_shape=pltpu.VMEM((16, 128), F32),
        compiler_params=params(16),
        cost_estimate=cost(27 * 10**8, 10**3),
    )(halo)


def row_latents(sums, part, halos, bias, placed, other_ends, token):
    clips, outs, cols, wide = sums.shape
    ch = wide // 2
    lanes = placed.shape[1]
    extra = [x for x in (other_ends, token) if x is not None]

    def kernel(s_ref, b_ref, p_ref, *refs):
        halo_refs, (o_ref, ends_ref, hidden) = refs[: len(halos)], refs[-3:]
        for c in range(clips):
            for t in range(outs):
                halo = halo_refs[c][t] if len(halos) == clips else halo_refs[0][c, t]
                at = (c * outs + t) * ch
                hidden[:, at : at + ch] = hidden_units(s_ref[c, t, :, part * ch : (part + 1) * ch], halo, b_ref[...])
        found = dot(hidden[...], p_ref[...])
        o_ref[:cols] = found
        o_ref[cols:] = jnp.zeros_like(o_ref[cols:])
        low = over_channels(jnp.min(found, axis=0, keepdims=True), jnp.minimum)
        high = over_channels(jnp.max(found, axis=0, keepdims=True), jnp.maximum)
        if other_ends is not None:
            other = refs[len(halos)]
            low, high = jnp.minimum(low, other[...]), jnp.maximum(high, other[...])
        ends_ref[...] = jnp.where(lax.broadcasted_iota(jnp.int32, (8, lanes), 0) == 0, low, high)

    args = [sums, bias, placed, *halos, *extra]
    return pl.pallas_call(
        kernel,
        in_specs=[IN_VMEM] * len(args),
        out_specs=[IN_VMEM] * 2,
        out_shape=[pltpu.VMEM((cols + 8, lanes), F32), pltpu.VMEM((8, lanes), F32)],
        scratch_shapes=[pltpu.VMEM((cols, clips * outs * ch), BF16)],
        compiler_params=params(16),
    )(*args)


def latent_messages(near, far, ends, other_ends, shards, copies):
    padded, lanes = near.shape
    half = lanes // 2
    share = (padded - 8) // shards

    def in_terms(x):
        first = x.astype(BF16).astype(F32)
        second = (x - first).astype(BF16).astype(F32)
        third = x - first - second
        block = lax.broadcasted_iota(jnp.int32, x.shape, 1) // (half // 4)
        return jnp.where(block == 4, first, jnp.where(block == 5, second, jnp.where(block == 6, third, 0.0)))

    def kernel(near_ref, far_ref, e_ref, other_ref, o_ref, latent):
        odd = odd_device()
        latent[1 - odd] = near_ref[...]
        latent[odd] = far_ref[...]
        lowest = jnp.minimum(e_ref[0:1], other_ref[0:1])
        highest = jnp.maximum(e_ref[1:2], other_ref[1:2])
        middle = (lowest + highest) * 0.5
        at_end = (lax.broadcasted_iota(jnp.int32, (8, lanes), 0) == 7) & (
            lax.broadcasted_iota(jnp.int32, (8, lanes), 1) >= half
        )
        in_front = lax.broadcasted_iota(jnp.int32, (8, lanes), 1) < half
        ends = (in_terms(lowest), in_terms(highest))
        for s in range(shards):
            rows = []
            for r in range(2):
                first = latent[r, pl.ds(share * s, 8)]
                second = latent[r, pl.ds(share * s + 8, 8)]
                rows.append(jnp.where(at_end, ends[r], jnp.where(in_front, first, second) - middle))
            message = jnp.concatenate(rows, axis=0).astype(BF16)
            for g in range(copies):
                o_ref[g, s] = message

    return pl.pallas_call(
        kernel,
        in_specs=[IN_VMEM] * 4,
        out_specs=IN_VMEM,
        out_shape=pltpu.VMEM((copies, shards, 16, lanes), BF16),
        scratch_shapes=[pltpu.VMEM((2, padded, lanes), F32)],
        compiler_params=params(16),
    )(near, far, ends, other_ends)


def coded_columns(received, share):
    groups, shards, _, lanes = received.shape
    latents = lanes // 8
    channels = lanes // 4

    def kernel(x_ref, o_ref, coded, turned):
        block = lax.broadcasted_iota(jnp.int32, (1, lanes), 1) // latents

        def end(g, row):
            terms = x_ref[g].astype(F32)[:, row, :]
            return terms + pltpu.roll(terms, lanes - latents, 1) + pltpu.roll(terms, lanes - 2 * latents, 1)

        def to_all(x):
            x = jnp.where(block == 4, x, 0.0)
            for step in (1, 2, 4):
                x = x + pltpu.roll(x, step * latents, 1)
            return x

        lows = [end(g, 7) for g in range(groups)]
        highs = [end(g, 15) for g in range(groups)]
        low = jnp.min(functools.reduce(jnp.minimum, lows), axis=0, keepdims=True)
        high = jnp.max(functools.reduce(jnp.maximum, highs), axis=0, keepdims=True)
        low, high = to_all(low), to_all(high)
        mine = lax.div(lax.axis_index("grp"), 2)
        middle = to_all((end(mine, 7) + end(mine, 15)) * 0.5)
        x = x_ref[mine].astype(F32) + middle[:, None, :]
        coded[...] = ((x - low) / (high - low) * 2.0 - 1.0).reshape(shards * 16, lanes)
        for first in range(8):
            piece_of = coded[pl.ds(first, 2 * shards, stride=8), :].T
            for piece in range(4):
                w, t = first + 8 * (piece // 2), piece % 2
                if w < share:
                    rows = piece_of[piece * channels : (piece + 1) * channels]
                    turned[pl.ds(2 * w + t, channels, stride=2 * share), :] = rows
        o_ref[...] = turned[...].astype(BF16)

    return pl.pallas_call(
        kernel,
        in_specs=[IN_VMEM],
        out_specs=IN_VMEM,
        out_shape=jax.ShapeDtypeStruct((channels * share * 2, 2 * shards), BF16),
        scratch_shapes=[pltpu.VMEM((shards * 16, lanes), F32), pltpu.VMEM((channels * share * 2, 2 * shards), F32)],
        compiler_params=params(16),
    )(in_vmem(received))


def on_device(frames, conv_weight, conv_bias, projection):
    clips, depth, rows, cols, ch = frames.shape
    latents = projection.shape[1]
    outs = depth - 2
    shards, groups = lax.axis_size("sp"), lax.axis_size("grp")
    share = cols // shards

    def swap(x, first):
        pairs = [(i, i + 1) for i in range(first, shards - 1, 2)]
        return lax.ppermute(x, "sp", pairs + [(b, a) for a, b in pairs])

    near_sums, far_sums0, near_taps, far_taps0, x1, far_w, inner, placed = first_edges(frames, conv_weight, projection.T)
    near, far0 = swap(near_sums, 0), swap(far_sums0, 1)
    far_sums1, far_taps1 = last_edges(x1, far_w)
    far1 = swap(far_sums1, 1)
    sums = inner_sums(near_taps, (far_taps0, far_taps1), inner)

    bias = conv_bias.reshape(1, ch)
    far_latents, far_ends = row_latents(sums, 1, (far0, far1), bias, placed, None, arrival(far0))
    near_latents, ends = row_latents(sums, 0, (near,), bias, placed, far_ends, None)
    other_ends = lax.ppermute(ends, "grp", [(i, i ^ 1) for i in range(groups)])
    messages = latent_messages(near_latents, far_latents, ends, other_ends, shards, groups // 2)
    messages = messages.reshape(groups // 2 * shards, 16, messages.shape[-1])
    same_core = [[(2 * y + core) * shards + s for y in range(groups // 2) for s in range(shards)] for core in range(2)]
    received = lax.all_to_all(messages, ("grp", "sp"), 0, 0, axis_index_groups=same_core)
    coded = coded_columns(received.reshape(groups // 2, shards, 16, -1), share)
    return coded.reshape(clips, latents, share, outs, rows * shards).transpose(0, 1, 3, 2, 4)


def solution(mesh):
    placed = (P("grp", None, "sp", None, None), P(), P(), P())
    return jax.shard_map(
        on_device,
        mesh=mesh,
        in_specs=placed,
        out_specs=P("grp", None, None, "sp", None),
        check_vma=False,
    )
```

```python
import functools

import jax
import jax.numpy as jnp
from jax import lax
from jax.experimental import pallas as pl
from jax.experimental.pallas import tpu as pltpu
from jax.sharding import PartitionSpec as P

F32, BF16 = jnp.float32, jnp.bfloat16
HBM, VMEM = pltpu.MemorySpace.HBM, pltpu.MemorySpace.VMEM
IN_HBM, IN_VMEM = pl.BlockSpec(memory_space=HBM), pl.BlockSpec(memory_space=VMEM)
DMA = pltpu.SemaphoreType.DMA


def dot(a, b):
    return jnp.dot(a, b, preferred_element_type=F32)


def cost(macs, nbytes):
    return pl.CostEstimate(flops=2 * macs, bytes_accessed=nbytes, transcendentals=0)


def params(mib):
    return pltpu.CompilerParams(vmem_limit_bytes=mib * 2**20)


def spread_taps(x, taps, at):
    cols, chans = x.shape
    wide = x.astype(F32)
    col = lax.broadcasted_iota(jnp.int32, wide.shape, 0)
    before = jnp.where(col == 0, 0.0, pltpu.roll(wide, 1, 0)).astype(BF16)
    after = jnp.where(col == cols - 1, 0.0, pltpu.roll(wide, cols - 1, 0)).astype(BF16)
    base = at * 3 * chans
    taps[:, base : base + chans] = before
    taps[:, base + chans : base + 2 * chans] = x
    taps[:, base + 2 * chans : base + 3 * chans] = after


def in_hbm(*arrays):
    return [pltpu.with_memory_space_constraint(x, HBM) for x in arrays]


def in_vmem(x):
    return pltpu.with_memory_space_constraint(x, VMEM)


def odd_device():
    return lax.rem(lax.axis_index("sp"), 2)


def edge_terms(taps, w, o_ref):
    ch = w.shape[1]

    def term(f, low, high):
        return dot(
            taps[:, f * 3 * ch : (f + 1) * 3 * ch],
            w[:, :, low * ch : high * ch].reshape(3 * ch, (high - low) * ch),
        )

    both = term(1, 1, 3) + term(2, 0, 2)
    o_ref[0] = (both[:, :ch] + term(0, 2, 3)).astype(BF16)
    o_ref[1] = (both[:, ch:] + term(3, 0, 1)).astype(BF16)


def first_edges(frames, weight, projection):
    clips, depth, _, cols, ch = frames.shape
    latents = projection.shape[0]

    def kernel(
        x_hbm, w_hbm, p_hbm, near_ref, far_ref, near_taps, far_taps, x1, far_w, inner, placed,
        x, w, p, x_sem, w_sem, i_sem, p_sem,
    ):
        odd = odd_device()
        in_p = pltpu.make_async_copy(p_hbm, p, p_sem)
        in_near = [pltpu.make_async_copy(x_hbm.at[c, :, 1 - odd], x.at[c], x_sem.at[c]) for c in range(clips)]
        in_far = pltpu.make_async_copy(x_hbm.at[0, :, odd], x.at[2], x_sem.at[2])
        in_far1 = pltpu.make_async_copy(x_hbm.at[1, :, odd], x1, x_sem.at[3])
        in_w, in_far_w = (
            [
                pltpu.make_async_copy(w_hbm.at[a, tap], to.at[:, :, pl.ds((2 - a) * ch, ch)], w_sem.at[e, a])
                for a in range(3)
            ]
            for e, (tap, to) in enumerate(((2 * odd, w), (2 - 2 * odd, far_w)))
        )
        in_inner = [
            pltpu.make_async_copy(w_hbm.at[a, b], inner.at[a, :, :, pl.ds(place * ch, ch)], i_sem.at[a, place])
            for a in range(3)
            for place, b in enumerate((2 * odd, 1, 2 - 2 * odd))
        ]
        in_near[0].start()
        for copy in in_w:
            copy.start()
        in_near[1].start()
        in_p.start()
        in_near[0].wait()
        for f in range(depth):
            spread_taps(x[0, f], near_taps.at[0], f)
        in_p.wait()
        k = lax.broadcasted_iota(jnp.int32, (latents, 128), 0)
        lane = lax.broadcasted_iota(jnp.int32, (latents, 128), 1)
        for c in range(clips):
            for t in range(2):
                pick = (lane % 64 == t * 32 + c * latents + k).astype(F32).astype(BF16)
                turned = lax.dot_general(p[...], pick, (((0,), (0,)), ((), ())), preferred_element_type=F32)
                at = (c * 2 + t) * ch
                placed[at : at + ch] = turned.astype(BF16)
        for copy in in_w:
            copy.wait()
        for copy in [in_far, *in_far_w, in_far1]:
            copy.start()
        edge_terms(near_taps.at[0], w, near_ref.at[0])
        in_near[1].wait()
        for f in range(depth):
            spread_taps(x[1, f], near_taps.at[1], f)
        for copy in in_inner:
            copy.start()
        edge_terms(near_taps.at[1], w, near_ref.at[1])
        in_far.wait()
        for f in range(depth):
            spread_taps(x[2, f], far_taps, f)
        for copy in in_far_w:
            copy.wait()
        edge_terms(far_taps, far_w, far_ref)
        for copy in [in_far1, *in_inner]:
            copy.wait()

    return pl.pallas_call(
        kernel,
        in_specs=[IN_HBM] * 3,
        out_specs=[IN_VMEM] * 8,
        out_shape=[
            pltpu.VMEM((clips, 2, cols, ch), BF16),
            pltpu.VMEM((2, cols, ch), BF16),
            pltpu.VMEM((clips, cols, depth * 3 * ch), BF16),
            pltpu.VMEM((cols, depth * 3 * ch), BF16),
            pltpu.VMEM((depth, cols, ch), BF16),
            pltpu.VMEM((3, ch, 3 * ch), BF16),
            pltpu.VMEM((3, 3, ch, 3 * ch), BF16),
            pltpu.VMEM((clips * 2 * ch, 128), BF16),
        ],
        scratch_shapes=[
            pltpu.VMEM((3, depth, cols, ch), BF16),
            pltpu.VMEM((3, ch, 3 * ch), BF16),
            pltpu.VMEM((latents, ch), BF16),
            DMA((4,)),
            DMA((2, 3)),
            DMA((3, 3)),
            DMA,
        ],
        compiler_params=params(16),
    )(*in_hbm(frames, weight, projection))


def last_edges(x1, edge_w):
    depth, cols, ch = x1.shape

    def kernel(x, w, o_ref, taps):
        for f in range(depth):
            spread_taps(x[f], taps, f)
        edge_terms(taps, w, o_ref)

    return pl.pallas_call(
        kernel,
        in_specs=[IN_VMEM] * 2,
        out_specs=[IN_VMEM] * 2,
        out_shape=[pltpu.VMEM((2, cols, ch), BF16), pltpu.VMEM((cols, depth * 3 * ch), BF16)],
        compiler_params=params(16),
    )(x1, edge_w)


def inner_sums(near, far, weight):
    clips, cols, _ = near.shape
    ch = weight.shape[2]

    def kernel(near, far0, far1, w, out):
        for c, far in enumerate((far0, far1)):
            for t in range(2):
                window = slice(t * 3 * ch, (t + 3) * 3 * ch)
                out[c, t] = dot(near[c, :, window], w[:, :, :, ch:].reshape(9 * ch, 2 * ch)) + dot(
                    far[:, window], w[:, :, :, : 2 * ch].reshape(9 * ch, 2 * ch)
                )

    return pl.pallas_call(
        kernel,
        in_specs=[IN_VMEM] * 4,
        out_specs=IN_VMEM,
        out_shape=pltpu.VMEM((clips, 2, cols, 2 * ch), F32),
        compiler_params=params(16),
    )(near, *far, weight)


def over_channels(x, pick):
    lanes = x.shape[1]
    x = pick(x, pltpu.roll(x, lanes // 8, 1))
    return pick(x, pltpu.roll(x, lanes // 4, 1))


def hidden_units(sums, halo, bias):
    h = (sums + halo.astype(F32) + bias) * 0.5
    return (h + h * jnp.tanh(h)).astype(BF16)


def arrival(halo):
    def kernel(x_ref, o_ref):
        o_ref[...] = x_ref[0, :16, :128].astype(F32)

    return pl.pallas_call(
        kernel,
        in_specs=[IN_VMEM],
        out_specs=IN_VMEM,
        out_shape=pltpu.VMEM((16, 128), F32),
        compiler_params=params(16),
        cost_estimate=cost(27 * 10**8, 10**3),
    )(halo)


def first_latents(sums, near, far0, bias, placed, token):
    clips, outs, cols, wide = sums.shape
    ch = wide // 2
    lanes = placed.shape[1]

    def kernel(s_ref, near_ref, far0_ref, b_ref, p_ref, _, near_out, far_out, ends_ref, hidden):
        for c in range(clips):
            for t in range(outs):
                at = (c * outs + t) * ch
                hidden[0, :, at : at + ch] = hidden_units(s_ref[c, t, :, :ch], near_ref[c, t], b_ref[...])
        for t in range(outs):
            hidden[1, :, t * ch : (t + 1) * ch] = hidden_units(s_ref[0, t, :, ch:], far0_ref[t], b_ref[...])
        found = dot(hidden[0], p_ref[...])
        near_out[:cols] = found
        near_out[cols:] = jnp.zeros_like(near_out[cols:])
        far_out[...] = dot(hidden[1, :, : outs * ch], p_ref[: outs * ch])
        low = over_channels(jnp.min(found, axis=0, keepdims=True), jnp.minimum)
        high = over_channels(jnp.max(found, axis=0, keepdims=True), jnp.maximum)
        ends_ref[...] = jnp.where(lax.broadcasted_iota(jnp.int32, (8, lanes), 0) == 0, low, high)

    return pl.pallas_call(
        kernel,
        in_specs=[IN_VMEM] * 6,
        out_specs=[IN_VMEM] * 3,
        out_shape=[pltpu.VMEM((cols + 8, lanes), F32), pltpu.VMEM((cols, lanes), F32), pltpu.VMEM((8, lanes), F32)],
        scratch_shapes=[pltpu.VMEM((2, cols, clips * outs * ch), BF16)],
        compiler_params=params(16),
    )(sums, near, far0, bias, placed, token)


def last_latents(sums, far1, bias, placed, far_latents0, near_ends):
    clips, outs, cols, wide = sums.shape
    ch = wide // 2
    lanes = placed.shape[1]

    def kernel(s_ref, far1_ref, b_ref, p_ref, far0_ref, near_ref, far_out, ends_ref, hidden):
        for t in range(outs):
            hidden[:, t * ch : (t + 1) * ch] = hidden_units(s_ref[1, t, :, ch:], far1_ref[t], b_ref[...])
        found = dot(hidden[...], p_ref[outs * ch :]) + far0_ref[...]
        far_out[:cols] = found
        far_out[cols:] = jnp.zeros_like(far_out[cols:])
        low = jnp.minimum(over_channels(jnp.min(found, axis=0, keepdims=True), jnp.minimum), near_ref[...])
        high = jnp.maximum(over_channels(jnp.max(found, axis=0, keepdims=True), jnp.maximum), near_ref[...])
        ends_ref[...] = jnp.where(lax.broadcasted_iota(jnp.int32, (8, lanes), 0) == 0, low, high)

    return pl.pallas_call(
        kernel,
        in_specs=[IN_VMEM] * 6,
        out_specs=[IN_VMEM] * 2,
        out_shape=[pltpu.VMEM((cols + 8, lanes), F32), pltpu.VMEM((8, lanes), F32)],
        scratch_shapes=[pltpu.VMEM((cols, outs * ch), BF16)],
        compiler_params=params(16),
    )(sums, far1, bias, placed, far_latents0, near_ends)


def latent_messages(near, far, ends, other_ends, shards, copies):
    padded, lanes = near.shape
    half = lanes // 2
    share = (padded - 8) // shards

    def in_terms(x):
        first = x.astype(BF16).astype(F32)
        second = (x - first).astype(BF16).astype(F32)
        third = x - first - second
        block = lax.broadcasted_iota(jnp.int32, x.shape, 1) // (half // 4)
        return jnp.where(block == 4, first, jnp.where(block == 5, second, jnp.where(block == 6, third, 0.0)))

    def kernel(near_ref, far_ref, e_ref, other_ref, o_ref, latent):
        odd = odd_device()
        latent[1 - odd] = near_ref[...]
        latent[odd] = far_ref[...]
        lowest = jnp.minimum(e_ref[0:1], other_ref[0:1])
        highest = jnp.maximum(e_ref[1:2], other_ref[1:2])
        middle = (lowest + highest) * 0.5
        at_end = (lax.broadcasted_iota(jnp.int32, (8, lanes), 0) == 7) & (
            lax.broadcasted_iota(jnp.int32, (8, lanes), 1) >= half
        )
        in_front = lax.broadcasted_iota(jnp.int32, (8, lanes), 1) < half
        ends = (in_terms(lowest), in_terms(highest))
        for s in range(shards):
            rows = []
            for r in range(2):
                first = latent[r, pl.ds(share * s, 8)]
                second = latent[r, pl.ds(share * s + 8, 8)]
                rows.append(jnp.where(at_end, ends[r], jnp.where(in_front, first, second) - middle))
            message = jnp.concatenate(rows, axis=0).astype(BF16)
            for g in range(copies):
                o_ref[g, s] = message

    return pl.pallas_call(
        kernel,
        in_specs=[IN_VMEM] * 4,
        out_specs=IN_VMEM,
        out_shape=pltpu.VMEM((copies, shards, 16, lanes), BF16),
        scratch_shapes=[pltpu.VMEM((2, padded, lanes), F32)],
        compiler_params=params(16),
    )(near, far, ends, other_ends)


def coded_columns(received, share):
    groups, shards, _, lanes = received.shape
    latents = lanes // 8
    channels = lanes // 4

    def kernel(x_ref, o_ref, coded, turned):
        block = lax.broadcasted_iota(jnp.int32, (1, lanes), 1) // latents

        def end(g, row):
            terms = x_ref[g].astype(F32)[:, row, :]
            return terms + pltpu.roll(terms, lanes - latents, 1) + pltpu.roll(terms, lanes - 2 * latents, 1)

        def to_all(x):
            x = jnp.where(block == 4, x, 0.0)
            for step in (1, 2, 4):
                x = x + pltpu.roll(x, step * latents, 1)
            return x

        lows = [end(g, 7) for g in range(groups)]
        highs = [end(g, 15) for g in range(groups)]
        low = jnp.min(functools.reduce(jnp.minimum, lows), axis=0, keepdims=True)
        high = jnp.max(functools.reduce(jnp.maximum, highs), axis=0, keepdims=True)
        low, high = to_all(low), to_all(high)
        mine = lax.div(lax.axis_index("grp"), 2)
        middle = to_all((end(mine, 7) + end(mine, 15)) * 0.5)
        x = x_ref[mine].astype(F32) + middle[:, None, :]
        coded[...] = ((x - low) / (high - low) * 2.0 - 1.0).reshape(shards * 16, lanes)
        for first in range(8):
            piece_of = coded[pl.ds(first, 2 * shards, stride=8), :].T
            for piece in range(4):
                w, t = first + 8 * (piece // 2), piece % 2
                if w < share:
                    rows = piece_of[piece * channels : (piece + 1) * channels]
                    turned[pl.ds(2 * w + t, channels, stride=2 * share), :] = rows
        o_ref[...] = turned[...].astype(BF16)

    return pl.pallas_call(
        kernel,
        in_specs=[IN_VMEM],
        out_specs=IN_VMEM,
        out_shape=jax.ShapeDtypeStruct((channels * share * 2, 2 * shards), BF16),
        scratch_shapes=[pltpu.VMEM((shards * 16, lanes), F32), pltpu.VMEM((channels * share * 2, 2 * shards), F32)],
        compiler_params=params(16),
    )(in_vmem(received))


def on_device(frames, conv_weight, conv_bias, projection):
    clips, depth, rows, cols, ch = frames.shape
    latents = projection.shape[1]
    outs = depth - 2
    shards, groups = lax.axis_size("sp"), lax.axis_size("grp")
    share = cols // shards

    def swap(x, first):
        pairs = [(i, i + 1) for i in range(first, shards - 1, 2)]
        return lax.ppermute(x, "sp", pairs + [(b, a) for a, b in pairs])

    near_sums, far_sums0, near_taps, far_taps0, x1, far_w, inner, placed = first_edges(frames, conv_weight, projection.T)
    near, far0 = swap(near_sums, 0), swap(far_sums0, 1)
    far_sums1, far_taps1 = last_edges(x1, far_w)
    far1 = swap(far_sums1, 1)
    sums = inner_sums(near_taps, (far_taps0, far_taps1), inner)

    bias = conv_bias.reshape(1, ch)
    near_latents, far_latents0, near_ends = first_latents(sums, near, far0, bias, placed, arrival(far0))
    far_latents, ends = last_latents(sums, far1, bias, placed, far_latents0, near_ends)
    other_ends = lax.ppermute(ends, "grp", [(i, i ^ 1) for i in range(groups)])
    messages = latent_messages(near_latents, far_latents, ends, other_ends, shards, groups // 2)
    messages = messages.reshape(groups // 2 * shards, 16, messages.shape[-1])
    same_core = [[(2 * y + core) * shards + s for y in range(groups // 2) for s in range(shards)] for core in range(2)]
    received = lax.all_to_all(messages, ("grp", "sp"), 0, 0, axis_index_groups=same_core)
    coded = coded_columns(received.reshape(groups // 2, shards, 16, -1), share)
    return coded.reshape(clips, latents, share, outs, rows * shards).transpose(0, 1, 3, 2, 4)


def solution(mesh):
    placed = (P("grp", None, "sp", None, None), P(), P(), P())
    return jax.shard_map(
        on_device,
        mesh=mesh,
        in_specs=placed,
        out_specs=P("grp", None, None, "sp", None),
        check_vma=False,
    )
```
